128 devices in a mesh: row: 8 (over x, core), col: 16 (over y, z).
Axes of the slice: x: 4, y: 4, z: 4, core: 2. Of those that a mesh axis runs over, the one named last changes fastest.
Arguments:
- inputs: bfloat16 [1024, 12288], P('row', 'col'), may hold values from -352 to 352
- w_up: bfloat16 [12288, 24576], P('col', 'row'), may hold values from -0.0546875 to 0.0546875
- bias_up: float32 [24576], P('row'), may hold values from -3 to 3
- w_down: bfloat16 [24576, 12288], P('row', 'col'), may hold values from -0.0390625 to 0.0390625
- bias_down: float32 [12288], P('col'), may hold values from -3 to 3
- student: float32 [1024, 12288], P('row', 'col'), may hold values from -352 to 352
Outputs:
- grad_inputs: float32 [1024, 12288], P('row', 'col')
- grad_up: bfloat16 [12288, 24576], P('col', 'row')
- grad_down: bfloat16 [24576, 12288], P('row', 'col')
The draws below stay inside these ranges and needn't reach their ends.
All inputs are finite; a program needn't handle non-finite values.
Results may differ from the reference program's by a relative error of at most 0.01.
Values may be sent and summed in bfloat16 or wider, within the bound.
No kernel may reach another device: no remote copies, remote signals or barrier semaphores. Data moves between devices by JAX's collectives and lax.ppermute only.
A program may use at most 192 MiB of HBM per device.

```python
import jax
import jax.numpy as jnp
from jax import lax

D = 12288
FF = 24576
TOKENS = 1024


def draw_inputs(key, part):
    key = jax.random.fold_in(key, 11)
    base_key = jax.random.fold_in(key, 0)
    values = jnp.clip(jax.random.normal(base_key, (TOKENS, D), jnp.float32), -4.0, 4.0)
    return values.astype(jnp.bfloat16)


def draw_student(key, part):
    key = jax.random.fold_in(key, 23)
    base_key = jax.random.fold_in(key, 0)
    values = jnp.clip(jax.random.normal(base_key, (TOKENS, D), jnp.float32), -4.0, 4.0)
    return values.astype(jnp.float32)


def block_levels(key, extent, pieces, smallest, largest):
    def one(dim, blocks):
        draws = jax.random.uniform(jax.random.fold_in(jax.random.fold_in(key, 6), dim), (blocks,), jnp.float32, smallest / len(pieces), largest / len(pieces))
        return jnp.repeat(jnp.exp(draws), extent[dim] // blocks).reshape((-1,) + (1,) * (len(extent) - dim - 1))

    loudness = one(*pieces[0])
    for cut in pieces[1:]:
        loudness = loudness * one(*cut)
    return loudness


def noise(key, shape, spread, bound, shards=(), kind=jnp.bfloat16):
    values = jax.random.normal(key, shape, jnp.float32) * spread
    if len(shards) > 0:
        values = block_levels(key, shape, shards, -0.22, 0.18) * values
    return jnp.clip(values, min=-bound, max=bound).astype(kind)


def setup_inputs(seed: int = 0) -> dict:
    streams_of = jax.random.split(jax.random.key(seed), 7)
    inputs = draw_inputs(jax.random.fold_in(streams_of[6], 71), 0)
    w_up = noise(streams_of[1], (D, FF), D ** -0.5, 0.0546875, ((0, 16), (1, 8)))
    bias_up = noise(streams_of[2], (FF,), 0.5, 3.0, ((0, 8),), jnp.float32)
    w_down = noise(streams_of[3], (FF, D), FF ** -0.5, 0.0390625, ((0, 8), (1, 16)))
    bias_down = noise(streams_of[4], (D,), 0.5, 3.0, ((0, 16),), jnp.float32)
    student = draw_student(jax.random.fold_in(streams_of[6], 71), 0)
    return {"inputs": inputs, "w_up": w_up, "bias_up": bias_up, "w_down": w_down, "bias_down": bias_down, "student": student}


def gelu_tanh(values):
    return jax.nn.gelu(values, approximate=True)

def reference(inputs, w_up, bias_up, w_down, bias_down, student):
    preact = jnp.dot(inputs, w_up, preferred_element_type=jnp.float32) + bias_up[None, :]
    hidden = gelu_tanh(preact).astype(jnp.bfloat16)
    mixed_out = jnp.dot(hidden, w_down, preferred_element_type=jnp.float32)
    logits = inputs.astype(jnp.float32) + mixed_out + bias_down[None, :]
    teacher_exp = jnp.exp(logits - lax.optimization_barrier(jnp.max(logits, axis=1, keepdims=True)))
    student_exp = jnp.exp(student - lax.optimization_barrier(jnp.max(student, axis=1, keepdims=True)))
    teacher_prob = teacher_exp / lax.optimization_barrier(jnp.sum(teacher_exp, axis=1, keepdims=True))
    student_prob = student_exp / lax.optimization_barrier(jnp.sum(student_exp, axis=1, keepdims=True))
    cotangent = (D * (teacher_prob - student_prob)).astype(jnp.bfloat16)
    grad_hidden = lax.dot_general(cotangent, w_down, (((1,), (1,)), ((), ())), preferred_element_type=jnp.float32)
    _, pullback = jax.vjp(gelu_tanh, preact)
    grad_pre = pullback(grad_hidden)[0].astype(jnp.bfloat16)
    grad_down = jnp.dot(hidden.T, cotangent, preferred_element_type=jnp.float32).astype(jnp.bfloat16)
    grad_up = jnp.dot(inputs.T, grad_pre, preferred_element_type=jnp.float32).astype(jnp.bfloat16)
    grad_inputs = cotangent.astype(jnp.float32) + jnp.dot(grad_pre, w_up.T, preferred_element_type=jnp.float32)
    return (grad_inputs, grad_up, grad_down)
```

```python
import jax
import jax.numpy as jnp
from jax import lax
from jax.sharding import PartitionSpec as P

D = 12288
BF = jnp.bfloat16
F32 = jnp.float32
F16 = jnp.float16
SIDE = 4
BOTH = ("row", "col")


def plane_perm(step_a, step_b):
    pairs = []
    for r in range(8):
        for c in range(16):
            a, b = (c // 4, c % 4) if r % 2 == 0 else (c % 4, c // 4)
            a, b = (a + step_a) % SIDE, (b + step_b) % SIDE
            to = a * 4 + b if r % 2 == 0 else b * 4 + a
            pairs.append((r * 16 + c, r * 16 + to))
    return pairs


def chip_perm(step):
    return [(r, (r + 2 * step) % 8) for r in range(8)]


PLANE_A = (BOTH, plane_perm(1, 0), plane_perm(-1, 0))
PLANE_B = (BOTH, plane_perm(0, 1), plane_perm(0, -1))
CHIPS = ("row", chip_perm(1), chip_perm(-1))
SWAP = [(r, r ^ 1) for r in range(8)]


def ring_scatter(part, ring, wire=(BF, 1.0)):
    axes, up, down = ring
    kind, scale = wire

    def pack(values):
        return (values * scale).astype(kind)

    def unpack(values):
        return values.astype(F32) * (1.0 / scale)

    far = pack(part(2))
    half = far.shape[0] // 2
    from_up = lax.ppermute(far[:half], axes, up)
    from_down = lax.ppermute(far[half:], axes, down)
    right, left = part(1), part(3)
    right = jnp.concatenate(
        [pack(right[:half] + unpack(from_up)), pack(right[half:])], 0
    )
    left = jnp.concatenate(
        [pack(left[:half]), pack(left[half:] + unpack(from_down))], 0
    )
    from_left = lax.ppermute(right, axes, up)
    from_right = lax.ppermute(left, axes, down)
    return part(0) + (unpack(from_left) + unpack(from_right))


def ring_gather(mine, ring):
    axes, up, down = ring
    half = mine.shape[0] // 2
    left = lax.ppermute(mine, axes, up)
    right = lax.ppermute(mine, axes, down)
    far_low = lax.ppermute(left[:half], axes, up)
    far_high = lax.ppermute(right[half:], axes, down)
    return [mine, right, jnp.concatenate([far_low, far_high], 0), left]


def in_order(blocks, place):
    joined = jnp.concatenate(blocks + blocks[:-1], 0)
    size = blocks[0].shape[0]
    start = ((SIDE - place) % SIDE) * size
    return lax.dynamic_slice_in_dim(joined, start, SIDE * size, 0)


def block_at(array, place, step):
    size = array.shape[0] // SIDE
    return lax.dynamic_slice_in_dim(array, ((place + step) % SIDE) * size, size, 0)


def plane_scatter(left, product, a, b, wire):
    held = {}

    def part(k):
        if k not in held:
            held[k] = lax.optimization_barrier(product(block_at(left, a, k)))
        return held[k]

    mine = ring_scatter(part, PLANE_A, wire)
    return ring_scatter(lambda k: block_at(mine, b, k), PLANE_B, wire)


def plane_gather(mine, a, b):
    return ring_gather(in_order(ring_gather(mine, PLANE_B), b), PLANE_A)


def row_gather(mine, x, core):
    own = in_order(ring_gather(mine, CHIPS), x)
    other = lax.ppermute(own, "row", SWAP)
    n = mine.shape[0]
    own, other = own.reshape(SIDE, 1, n, -1), other.reshape(SIDE, 1, n, -1)
    first = jnp.where(core == 0, own, other)
    second = jnp.where(core == 0, other, own)
    return jnp.concatenate([first, second], 1).reshape(8 * n, -1)


def row_scatter(parts, x, core, wire):
    n = parts.shape[0] // 8
    parts = parts.reshape(SIDE, 2, n, -1)
    own = lax.dynamic_index_in_dim(parts, core, 1, False).reshape(SIDE * n, -1)
    other = lax.dynamic_index_in_dim(parts, 1 - core, 1, False).reshape(SIDE * n, -1)
    kind, scale = wire
    got = lax.ppermute((other * scale).astype(kind), "row", SWAP)
    own = own.astype(F32) + got.astype(F32) * (1.0 / scale)
    return ring_scatter(lambda k: block_at(own, x, k), CHIPS, wire)


def gelu_tanh(values):
    return jax.nn.gelu(values, approximate=True)


def rows_by(left, right):
    return jnp.dot(left, right, preferred_element_type=F32)


def against_rows(left, right):
    return lax.dot_general(left, right, (((1,), (1,)), ((), ())), preferred_element_type=F32)


def over_tokens(left, right):
    return lax.dot_general(left, right, (((0,), (0,)), ((), ())), preferred_element_type=F32)


def local(inputs, w_up, bias_up, w_down, bias_down, student):
    row, col = lax.axis_index("row"), lax.axis_index("col")
    x, core = row // 2, row % 2
    y, z = col // 4, col % 4
    a = jnp.where(core == 0, y, z)
    b = jnp.where(core == 0, z, y)

    gathered = row_gather(inputs, x, core)
    preact = plane_scatter(gathered, lambda left: rows_by(left, w_up), a, b, (F16, 2.0**-1)) + bias_up[None, :]
    hidden_mine = gelu_tanh(preact).astype(BF)
    hidden = plane_gather(hidden_mine, a, b)
    mixed = in_order([rows_by(block, w_down) for block in hidden], a)
    mixed_out = row_scatter(mixed, x, core, (F16, 2.0**-11))
    logits = inputs.astype(F32) + mixed_out + bias_down[None, :]

    def stats(values):
        peak = jnp.max(values, axis=1)
        return peak, jnp.sum(jnp.exp(values - peak[:, None]), axis=1)

    n = inputs.shape[0]
    sent = jnp.stack([*stats(logits), *stats(student)])
    sent = jnp.broadcast_to(sent[None], (16, 4, n))
    seen = lax.all_to_all(sent, "col", 0, 0, tiled=True)
    peaks_t, sums_t, peaks_s, sums_s = seen[:, 0], seen[:, 1], seen[:, 2], seen[:, 3]

    def probability(values, peaks, sums):
        peak = jnp.max(peaks, axis=0)
        mass = jnp.sum(sums * jnp.exp(peaks - peak[None, :]), axis=0)
        return jnp.exp(values - peak[:, None]) / mass[:, None]

    teacher_prob = probability(logits, peaks_t, sums_t)
    student_prob = probability(student, peaks_s, sums_s)
    cotangent = (D * (teacher_prob - student_prob)).astype(BF)
    slopes = row_gather(cotangent, x, core)

    grad_hidden = plane_scatter(slopes, lambda left: against_rows(left, w_down), a, b, (F16, 2.0**5))
    _, pullback = jax.vjp(gelu_tanh, preact)
    grad_pre_mine = pullback(grad_hidden)[0].astype(BF)
    hidden_all = in_order(hidden, a)
    grad_down = over_tokens(hidden_all, slopes).astype(BF)
    grad_pre = plane_gather(grad_pre_mine, a, b)
    back = in_order([against_rows(block, w_up).astype(BF) for block in grad_pre], a)
    grad_inputs = cotangent.astype(F32) + row_scatter(back, x, core, (BF, 1.0))
    grad_up = over_tokens(gathered, in_order(grad_pre, a)).astype(BF)
    return (grad_inputs, grad_up, grad_down)


def solution(mesh):
    return jax.shard_map(
        local,
        mesh=mesh,
        in_specs=(
            P("row", "col"),
            P("col", "row"),
            P("row"),
            P("row", "col"),
            P("col"),
            P("row", "col"),
        ),
        out_specs=(P("row", "col"), P("col", "row"), P("row", "col")),
        check_vma=False,
    )
```

```python
import jax
import jax.numpy as jnp
from jax import lax
from jax.experimental import pallas as pl
from jax.experimental.pallas import tpu as pltpu
from jax.sharding import PartitionSpec as P

D = 12288
BF = jnp.bfloat16
F16 = jnp.float16
F32 = jnp.float32
SIDE = 4
HALVES = 2
BOTH = ("row", "col")


def plane_perm(step_a, step_b):
    pairs = []
    for r in range(8):
        for c in range(16):
            a, b = (c // 4, c % 4) if r % 2 == 0 else (c % 4, c // 4)
            a, b = (a + step_a) % SIDE, (b + step_b) % SIDE
            to = a * 4 + b if r % 2 == 0 else b * 4 + a
            pairs.append((r * 16 + c, r * 16 + to))
    return pairs


def chip_perm(step):
    return [(r, (r + 2 * step) % 8) for r in range(8)]


PLANE_A = (BOTH, plane_perm(1, 0), plane_perm(-1, 0))
PLANE_FAR = plane_perm(0, 2)
PLANE_B = (BOTH, plane_perm(0, 1), plane_perm(0, -1))
CHIPS = ("row", chip_perm(1), chip_perm(-1))
SWAP = [(r, r ^ 1) for r in range(8)]


def packer(kind, scale):
    def pack(values):
        return (values * scale).astype(kind)

    def unpack(values):
        return values.astype(F32) * (1.0 / scale)

    return pack, unpack


PREACT_WIRE = packer(F16, 2.0**-1)
MIXED_WIRE = packer(F16, 2.0**-11)
GRAD_WIRE = packer(F16, 2.0**5)
BACK_WIRE = packer(BF, 1.0)


def ring_first(far, ring):
    axes, up, down = ring
    half = far.shape[0] // 2
    return lax.ppermute(far[:half], axes, up), lax.ppermute(far[half:], axes, down)


def ring_pair(right, left, arrived, wire):
    pack, unpack = wire
    from_up, from_down = arrived
    half = right.shape[0] // 2
    right = jnp.concatenate([pack(unpack(right[:half]) + unpack(from_up)), right[half:]], 0)
    left = jnp.concatenate([left[:half], pack(unpack(left[half:]) + unpack(from_down))], 0)
    return right, left


def ring_send(pair, ring):
    axes, up, down = ring
    return lax.ppermute(pair[0], axes, up), lax.ppermute(pair[1], axes, down)


def ring_second(right, left, arrived, ring, wire):
    return ring_send(ring_pair(right, left, arrived, wire), ring)


def ring_total(own, arrived, wire):
    _, unpack = wire
    return unpack(own) + (unpack(arrived[0]) + unpack(arrived[1]))


def ring_scatter(parts, ring, wire):
    own, right, far, left = parts
    arrived = ring_second(right, left, ring_first(far, ring), ring, wire)
    return ring_total(own, arrived, wire)


def ring_gather(mine, ring, before=None):
    axes, up, down = ring
    half = mine.shape[0] // 2
    left = lax.ppermute(mine, axes, up)
    right = lax.ppermute(mine, axes, down)
    if before is not None:
        left, right, before = lax.optimization_barrier((left, right, before))
    far_low = lax.ppermute(left[:half], axes, up)
    far_high = lax.ppermute(right[half:], axes, down)
    return [mine, right, far_low, far_high, left], before


def quarters(array):
    size = array.shape[0] // SIDE
    return [array[k * size : (k + 1) * size] for k in range(SIDE)]


def join(lines):
    pieces = [piece for line in lines for piece in line]

    def kernel(*refs):
        top, k = 0, 0
        for line in lines:
            side = 0
            for piece in line:
                height, width = piece.shape
                refs[-1][top : top + height, side : side + width] = refs[k][...]
                side, k = side + width, k + 1
            top += line[0].shape[0]

    total = sum(line[0].shape[0] for line in lines)
    width = sum(piece.shape[1] for piece in lines[0])
    return pl.pallas_call(
        kernel,
        out_shape=jax.ShapeDtypeStruct((total, width), pieces[0].dtype),
        in_specs=[pl.BlockSpec(memory_space=pltpu.VMEM)] * len(pieces),
        out_specs=pl.BlockSpec(memory_space=pltpu.VMEM),
        compiler_params=pltpu.CompilerParams(vmem_limit_bytes=24 * 2**20),
    )(*pieces)


def arrange(pieces, places, size):
    width = pieces[0].shape[1]
    total = sum(piece.shape[0] for piece in pieces)

    def kernel(places_ref, *refs):
        out = refs[-1]
        block = 0
        for ref in refs[:-1]:
            for start in range(0, ref.shape[0], size):
                at = pl.multiple_of(places_ref[block] * size, size)
                out[pl.ds(at, size), :] = ref[start : start + size, :]
                block += 1

    return pl.pallas_call(
        kernel,
        out_shape=jax.ShapeDtypeStruct((total, width), pieces[0].dtype),
        in_specs=[pl.BlockSpec(memory_space=pltpu.SMEM)]
        + [pl.BlockSpec(memory_space=pltpu.VMEM)] * len(pieces),
        out_specs=pl.BlockSpec(memory_space=pltpu.VMEM),
        compiler_params=pltpu.CompilerParams(vmem_limit_bytes=24 * 2**20),
    )(places, *pieces)


def columns(array):
    size = array.shape[1] // HALVES
    return [array[:, c * size : (c + 1) * size] for c in range(HALVES)]


def plane_scatter(left, product, wire):
    pack, unpack = wire
    axes, up, down = PLANE_A
    blocks = quarters(left)
    far = pack(product(blocks[2]))
    half = far.shape[0] // 2
    low, high = columns(far[:half]), columns(far[half:])
    low, high, others = lax.optimization_barrier((low, high, [blocks[1], blocks[3], blocks[0]]))
    first = [(lax.ppermute(l, axes, up), lax.ppermute(h, axes, down)) for l, h in zip(low, high)]
    right, left, own = [columns(pack(product(block))) for block in others]
    second = [
        ring_second(right[c], left[c], first[c], PLANE_A, wire) for c in range(HALVES)
    ]
    sums, parts = [], None
    for c in range(HALVES):
        here = second[c]
        if parts is not None:
            here, _ = lax.optimization_barrier((here, parts))
        parts = [pack(block) for block in quarters(ring_total(own[c], here, wire))]
        _, up, down = PLANE_B
        arrived = [
            lax.ppermute(parts[k], BOTH, p) for k, p in ((2, PLANE_FAR), (1, up), (3, down))
        ]
        sums.append(unpack(parts[0]) + (unpack(arrived[0]) + (unpack(arrived[1]) + unpack(arrived[2]))))
    return sums


def plane_gather(mines, before=None):
    spans = []
    for mine in mines:
        _, up, down = PLANE_B
        far = lax.ppermute(mine, BOTH, PLANE_FAR)
        left, right = lax.ppermute(mine, BOTH, up), lax.ppermute(mine, BOTH, down)
        blocks = [mine, right, far, left]
        blocks, before = ring_gather(join([[block] for block in blocks]), PLANE_A, before)
        spans.append(blocks)
    own, right, low, high, left = zip(*spans)
    return [join([own]), join([right]), join([low, high]), join([left])], before


class Place:
    def __init__(self):
        row, col = lax.axis_index("row"), lax.axis_index("col")
        self.x, self.core = row // 2, row % 2
        y, z = col // 4, col % 4
        self.a = jnp.where(self.core == 0, y, z)
        self.b = jnp.where(self.core == 0, z, y)
        steps = jnp.arange(SIDE)
        halves = jnp.arange(2)

        def gather_places(core):
            step_a = (self.x + steps[:, None] - self.a + SIDE) % SIDE
            step_b = (2 * core + halves[None, :] - self.b + SIDE) % SIDE
            return (step_a * SIDE + step_b).reshape(-1)

        self.gather = jnp.concatenate(
            [gather_places(self.core), gather_places(1 - self.core)]
        ).astype(jnp.int32)
        at_a = (self.a + steps[:, None]) % SIDE
        at_b = (self.b + steps[None, :]) % SIDE
        chip = (at_a - self.x + SIDE) % SIDE
        self.scatter = (
            jnp.where(at_b // 2 == self.core, 0, 8) + chip * 2 + at_b % 2
        ).reshape(-1).astype(jnp.int32)


def row_gather(mine, place):
    own, _ = ring_gather(mine, CHIPS)
    other = lax.ppermute(jnp.concatenate(own, 0), "row", SWAP)
    return arrange(own + [other], place.gather, mine.shape[0] // 2)


def row_scatter(pieces, place, wire):
    pack, unpack = wire
    total = sum(piece.shape[0] for piece in pieces)
    placed = arrange(pieces, place.scatter, total // 16)
    own, other = placed[: total // 2], placed[total // 2 :]
    got = lax.ppermute(pack(other), "row", SWAP)
    own = pack(own.astype(F32) + unpack(got))
    return ring_scatter(quarters(own), CHIPS, wire)


def gelu_tanh(values):
    return jax.nn.gelu(values, approximate=True)


def rows_by(left, right):
    return jnp.dot(left, right, preferred_element_type=F32)


def against_rows(left, right):
    return lax.dot_general(left, right, (((1,), (1,)), ((), ())), preferred_element_type=F32)


def over_tokens(left, right):
    return lax.dot_general(left, right, (((0,), (0,)), ((), ())), preferred_element_type=F32)


def probabilities_difference(logits, student):
    def stats(values):
        peak = jnp.max(values, axis=1)
        return peak, jnp.sum(jnp.exp(values - peak[:, None]), axis=1)

    n = logits.shape[0]
    sent = jnp.stack([*stats(logits), *stats(student)])
    sent = jnp.broadcast_to(sent[None], (16, 4, n))
    seen = lax.all_to_all(sent, "col", 0, 0, tiled=True)

    def probability(values, peaks, sums):
        peak = jnp.max(peaks, axis=0)
        mass = jnp.sum(sums * jnp.exp(peaks - peak[None, :]), axis=0)
        return jnp.exp(values - peak[:, None]) / mass[:, None]

    return probability(logits, seen[:, 0], seen[:, 1]) - probability(student, seen[:, 2], seen[:, 3])


def local(inputs, w_up, bias_up, w_down, bias_down, student):
    place = Place()
    tokens = row_gather(inputs, place)
    preact = plane_scatter(tokens, lambda left: rows_by(left, w_up), PREACT_WIRE)
    preact = [part + bias for part, bias in zip(preact, columns(bias_up[None, :]))]
    hidden, _ = plane_gather([gelu_tanh(part).astype(BF) for part in preact])
    mixed_out = row_scatter([rows_by(block, w_down) for block in hidden], place, MIXED_WIRE)
    logits = inputs.astype(F32) + mixed_out + bias_down[None, :]
    cotangent = (D * probabilities_difference(logits, student)).astype(BF)
    slopes = row_gather(cotangent, place)
    grad_hidden = plane_scatter(slopes, lambda left: against_rows(left, w_down), GRAD_WIRE)
    grad_pre = [
        jax.vjp(gelu_tanh, part)[1](grad)[0].astype(BF) for part, grad in zip(preact, grad_hidden)
    ]
    grad_down = over_tokens(jnp.concatenate(hidden, 0), slopes).astype(BF)
    grad_pre, grad_down = plane_gather(grad_pre, grad_down)
    back = [against_rows(block, w_up).astype(BF) for block in grad_pre]
    grad_inputs = cotangent.astype(F32) + row_scatter(back, place, BACK_WIRE)
    grad_up = over_tokens(tokens, jnp.concatenate(grad_pre, 0)).astype(BF)
    return (grad_inputs, grad_up, grad_down)


def solution(mesh):
    return jax.shard_map(
        local,
        mesh=mesh,
        in_specs=(
            P("row", "col"),
            P("col", "row"),
            P("row"),
            P("row", "col"),
            P("col"),
            P("row", "col"),
        ),
        out_specs=(P("row", "col"), P("col", "row"), P("row", "col")),
        check_vma=False,
    )
```

```python
import jax
import jax.numpy as jnp
from jax import lax
from jax.experimental import pallas as pl
from jax.experimental.pallas import tpu as pltpu
from jax.sharding import PartitionSpec as P

D = 12288
BF = jnp.bfloat16
F16 = jnp.float16
F32 = jnp.float32
SIDE = 4
HALVES = 2
BOTH = ("row", "col")


def plane_perm(step_a, step_b):
    pairs = []
    for r in range(8):
        for c in range(16):
            a, b = (c // 4, c % 4) if r % 2 == 0 else (c % 4, c // 4)
            a, b = (a + step_a) % SIDE, (b + step_b) % SIDE
            to = a * 4 + b if r % 2 == 0 else b * 4 + a
            pairs.append((r * 16 + c, r * 16 + to))
    return pairs


def chip_perm(step):
    return [(r, (r + 2 * step) % 8) for r in range(8)]


PLANE_A = (BOTH, plane_perm(1, 0), plane_perm(-1, 0))
PLANE_FAR = plane_perm(0, 2)
PLANE_B = (BOTH, plane_perm(0, 1), plane_perm(0, -1))
CHIPS = ("row", chip_perm(1), chip_perm(-1))
SWAP = [(r, r ^ 1) for r in range(8)]


def packer(kind, scale):
    def pack(values):
        return (values * scale).astype(kind)

    def unpack(values):
        return values.astype(F32) * (1.0 / scale)

    return pack, unpack


PREACT_WIRE = packer(F16, 2.0**-1)
MIXED_WIRE = packer(F16, 2.0**-11)
GRAD_WIRE = packer(F16, 2.0**5)
BACK_WIRE = packer(BF, 1.0)


def ring_first(far, ring):
    axes, up, down = ring
    half = far.shape[0] // 2
    return lax.ppermute(far[:half], axes, up), lax.ppermute(far[half:], axes, down)


def ring_pair(right, left, arrived, wire):
    pack, unpack = wire
    from_up, from_down = arrived
    half = right.shape[0] // 2
    right = jnp.concatenate([pack(unpack(right[:half]) + unpack(from_up)), right[half:]], 0)
    left = jnp.concatenate([left[:half], pack(unpack(left[half:]) + unpack(from_down))], 0)
    return right, left


def ring_send(pair, ring):
    axes, up, down = ring
    return lax.ppermute(pair[0], axes, up), lax.ppermute(pair[1], axes, down)


def ring_total(own, arrived, wire):
    _, unpack = wire
    return unpack(own) + (unpack(arrived[0]) + unpack(arrived[1]))


def ring_scatter(parts, ring, wire):
    own, right, far, left = parts
    arrived = ring_send(ring_pair(right, left, ring_first(far, ring), wire), ring)
    return ring_total(own, arrived, wire)


def ring_gather(mine, ring):
    axes, up, down = ring
    half = mine.shape[0] // 2
    left = lax.ppermute(mine, axes, up)
    right = lax.ppermute(mine, axes, down)
    far_low = lax.ppermute(left[:half], axes, up)
    far_high = lax.ppermute(right[half:], axes, down)
    return [mine, right, far_low, far_high, left]


def quarters(array):
    size = array.shape[0] // SIDE
    return [array[k * size : (k + 1) * size] for k in range(SIDE)]


def join(lines):
    pieces = [piece for line in lines for piece in line]

    def kernel(*refs):
        top, k = 0, 0
        for line in lines:
            side = 0
            for piece in line:
                height, width = piece.shape
                refs[-1][top : top + height, side : side + width] = refs[k][...]
                side, k = side + width, k + 1
            top += line[0].shape[0]

    total = sum(line[0].shape[0] for line in lines)
    width = sum(piece.shape[1] for piece in lines[0])
    return pl.pallas_call(
        kernel,
        out_shape=jax.ShapeDtypeStruct((total, width), pieces[0].dtype),
        in_specs=[pl.BlockSpec(memory_space=pltpu.VMEM)] * len(pieces),
        out_specs=pl.BlockSpec(memory_space=pltpu.VMEM),
        compiler_params=pltpu.CompilerParams(vmem_limit_bytes=24 * 2**20),
    )(*pieces)


def arrange(pieces, places, which, size):
    width = pieces[0].shape[1]
    total = sum(piece.shape[0] for piece in pieces)

    def kernel(places_ref, *refs):
        out = refs[-1]
        block = 0
        for ref in refs[:-1]:
            for start in range(0, ref.shape[0], size):
                at = pl.multiple_of(places_ref[which, block] * size, size)
                out[pl.ds(at, size), :] = ref[start : start + size, :]
                block += 1

    return pl.pallas_call(
        kernel,
        out_shape=jax.ShapeDtypeStruct((total, width), pieces[0].dtype),
        in_specs=[pl.BlockSpec(memory_space=pltpu.SMEM)]
        + [pl.BlockSpec(memory_space=pltpu.VMEM)] * len(pieces),
        out_specs=pl.BlockSpec(memory_space=pltpu.VMEM),
        compiler_params=pltpu.CompilerParams(vmem_limit_bytes=24 * 2**20),
    )(places, *pieces)


def columns(array):
    size = array.shape[1] // HALVES
    return [array[:, c * size : (c + 1) * size] for c in range(HALVES)]


def after(values, done):
    return lax.optimization_barrier((values, done))[0]


def cut(left, right):
    half = left.shape[0] // 2

    def kernel(left_ref, right_ref, low_ref, high_ref):
        low_ref[...] = left_ref[:half, :]
        high_ref[...] = right_ref[half:, :]

    piece = jax.ShapeDtypeStruct((half, left.shape[1]), left.dtype)
    return pl.pallas_call(
        kernel,
        out_shape=[piece, piece],
        in_specs=[pl.BlockSpec(memory_space=pltpu.VMEM)] * 2,
        out_specs=[pl.BlockSpec(memory_space=pltpu.VMEM)] * 2,
        compiler_params=pltpu.CompilerParams(vmem_limit_bytes=24 * 2**20),
    )(left, right)


def plane_scatter(left, product, wire):
    pack, unpack = wire
    axes, up, down = PLANE_A
    blocks = quarters(left)
    far = pack(product(blocks[2]))
    half = far.shape[0] // 2
    low, high = lax.optimization_barrier((columns(far[:half]), columns(far[half:])))
    first = [(lax.ppermute(l, axes, up), lax.ppermute(h, axes, down)) for l, h in zip(low, high)]
    near = after((blocks[1], blocks[3]), low)
    right, left = [columns(pack(product(block))) for block in near]
    pairs = []
    for c in range(HALVES):
        came = first[c]
        if c:
            came = after(came, pairs[0])
        pairs.append(ring_pair(right[c], left[c], came, wire))
    second = [ring_send(pair, PLANE_A) for pair in pairs]
    own = columns(pack(product(after(blocks[0], pairs[1]))))
    sums, parts = [], None
    for c in range(HALVES):
        here = second[c]
        if parts is not None:
            here = after(here, parts)
        parts = [pack(block) for block in quarters(ring_total(own[c], here, wire))]
        _, up, down = PLANE_B
        arrived = [
            lax.ppermute(parts[k], BOTH, p) for k, p in ((2, PLANE_FAR), (1, up), (3, down))
        ]
        sums.append(unpack(parts[0]) + (unpack(arrived[0]) + (unpack(arrived[1]) + unpack(arrived[2]))))
    return sums


def plane_gather(mines, product, extra=None):
    owns, lefts, rights, halves = [], [], [], []
    axes, up, down = PLANE_A
    for mine in mines:
        far = lax.ppermute(mine, BOTH, PLANE_FAR)
        left, right = lax.ppermute(mine, BOTH, PLANE_B[1]), lax.ppermute(mine, BOTH, PLANE_B[2])
        owns.append(join([[mine], [right], [far], [left]]))
        lefts.append(lax.ppermute(owns[-1], axes, up))
        rights.append(lax.ppermute(owns[-1], axes, down))
        if extra is not None:
            lefts[-1], rights[-1], extra = lax.optimization_barrier((lefts[-1], rights[-1], extra))
        halves.append(cut(lefts[-1], rights[-1]))
    fars = [(lax.ppermute(l, axes, up), lax.ppermute(h, axes, down)) for l, h in halves]
    own = join([owns])
    product_own = product(own)
    lefts, rights = after((lefts, rights), halves[1])
    right, left = join([rights]), join([lefts])
    product_right, product_left = product(right), product(left)
    far = join(list(zip(*fars)))
    blocks = [own, right, far, left]
    return blocks, [product_own, product_right, product(far), product_left], extra


class Place:
    def __init__(self):
        row, col = lax.axis_index("row"), lax.axis_index("col")
        self.x, self.core = row // 2, row % 2
        y, z = col // 4, col % 4
        self.a = jnp.where(self.core == 0, y, z)
        self.b = jnp.where(self.core == 0, z, y)
        steps = jnp.arange(SIDE)
        halves = jnp.arange(2)

        def gather_places(core):
            step_a = (self.x + steps[:, None] - self.a + SIDE) % SIDE
            step_b = (2 * core + halves[None, :] - self.b + SIDE) % SIDE
            return (step_a * SIDE + step_b).reshape(-1)

        gather = jnp.concatenate([gather_places(self.core), gather_places(1 - self.core)])
        at_a = (self.a + steps[:, None]) % SIDE
        at_b = (self.b + steps[None, :]) % SIDE
        chip = (at_a - self.x + SIDE) % SIDE
        scatter = jnp.where(at_b // 2 == self.core, 0, 8) + chip * 2 + at_b % 2
        self.table = lax.optimization_barrier(
            jnp.stack([gather, scatter.reshape(-1)]).astype(jnp.int32)
        )


def row_gather(mine, place):
    own = ring_gather(mine, CHIPS)
    other = lax.ppermute(jnp.concatenate(own, 0), "row", SWAP)
    return arrange(own + [other], place.table, 0, mine.shape[0] // 2)


def row_scatter(pieces, place, wire):
    pack, unpack = wire
    total = sum(piece.shape[0] for piece in pieces)
    placed = arrange(pieces, place.table, 1, total // 16)
    own, other = placed[: total // 2], placed[total // 2 :]
    got = lax.ppermute(pack(other), "row", SWAP)
    own = pack(own.astype(F32) + unpack(got))
    return ring_scatter(quarters(own), CHIPS, wire)


def gelu_tanh(values):
    return jax.nn.gelu(values, approximate=True)


def rows_by(left, right):
    return jnp.dot(left, right, preferred_element_type=F32)


def against_rows(left, right):
    return lax.dot_general(left, right, (((1,), (1,)), ((), ())), preferred_element_type=F32)


def over_tokens(left, right):
    return lax.dot_general(left, right, (((0,), (0,)), ((), ())), preferred_element_type=F32)


def probabilities_difference(logits, student):
    def stats(values):
        peak = jnp.max(values, axis=1)
        return peak, jnp.sum(jnp.exp(values - peak[:, None]), axis=1)

    n = logits.shape[0]
    sent = jnp.stack([*stats(logits), *stats(student)])
    sent = jnp.broadcast_to(sent[None], (16, 4, n))
    seen = lax.all_to_all(sent, "col", 0, 0, tiled=True)

    def probability(values, peaks, sums):
        peak = jnp.max(peaks, axis=0)
        mass = jnp.sum(sums * jnp.exp(peaks - peak[None, :]), axis=0)
        return jnp.exp(values - peak[:, None]) / mass[:, None]

    return probability(logits, seen[:, 0], seen[:, 1]) - probability(student, seen[:, 2], seen[:, 3])


def local(inputs, w_up, bias_up, w_down, bias_down, student):
    place = Place()
    tokens = row_gather(inputs, place)
    preact = plane_scatter(tokens, lambda left: rows_by(left, w_up), PREACT_WIRE)
    preact = [part + bias for part, bias in zip(preact, columns(bias_up[None, :]))]
    hidden, mixed, _ = plane_gather(
        [gelu_tanh(part).astype(BF) for part in preact], lambda left: rows_by(left, w_down)
    )
    mixed_out = row_scatter(mixed, place, MIXED_WIRE)
    logits = inputs.astype(F32) + mixed_out + bias_down[None, :]
    cotangent = (D * probabilities_difference(logits, student)).astype(BF)
    slopes = row_gather(cotangent, place)
    grad_hidden = plane_scatter(slopes, lambda left: against_rows(left, w_down), GRAD_WIRE)
    grad_down = over_tokens(jnp.concatenate(hidden, 0), slopes).astype(BF)
    grad_pre = [
        jax.vjp(gelu_tanh, part)[1](grad)[0].astype(BF) for part, grad in zip(preact, grad_hidden)
    ]
    grad_pre, back, grad_down = plane_gather(
        grad_pre, lambda left: against_rows(left, w_up).astype(BF), grad_down
    )
    grad_inputs = cotangent.astype(F32) + row_scatter(back, place, BACK_WIRE)
    grad_up = over_tokens(tokens, jnp.concatenate(grad_pre, 0)).astype(BF)
    return (grad_inputs, grad_up, grad_down)


def solution(mesh):
    return jax.shard_map(
        local,
        mesh=mesh,
        in_specs=(
            P("row", "col"),
            P("col", "row"),
            P("row"),
            P("row", "col"),
            P("col"),
            P("row", "col"),
        ),
        out_specs=(P("row", "col"), P("col", "row"), P("row", "col")),
        check_vma=False,
    )
```

```python
import jax
import jax.numpy as jnp
from jax import lax
from jax.experimental import pallas as pl
from jax.experimental.pallas import tpu as pltpu
from jax.sharding import PartitionSpec as P

D = 12288
BF = jnp.bfloat16
F16 = jnp.float16
F32 = jnp.float32
SIDE = 4
HALVES = 2
BOTH = ("row", "col")


def plane_perm(step_a, step_b):
    pairs = []
    for r in range(8):
        for c in range(16):
            a, b = (c // 4, c % 4) if r % 2 == 0 else (c % 4, c // 4)
            a, b = (a + step_a) % SIDE, (b + step_b) % SIDE
            to = a * 4 + b if r % 2 == 0 else b * 4 + a
            pairs.append((r * 16 + c, r * 16 + to))
    return pairs


def chip_perm(step):
    return [(r, (r + 2 * step) % 8) for r in range(8)]


PLANE_A = (BOTH, plane_perm(1, 0), plane_perm(-1, 0))
PLANE_FAR = plane_perm(0, 2)
PLANE_B = (BOTH, plane_perm(0, 1), plane_perm(0, -1))
CHIPS = ("row", chip_perm(1), chip_perm(-1))
SWAP = [(r, r ^ 1) for r in range(8)]


def packer(kind, scale):
    def pack(values):
        return (values * scale).astype(kind)

    def unpack(values):
        return values.astype(F32) * (1.0 / scale)

    return pack, unpack


PREACT_WIRE = packer(F16, 2.0**-1)
MIXED_WIRE = packer(F16, 2.0**-11)
GRAD_WIRE = packer(F16, 2.0**5)
BACK_WIRE = packer(BF, 1.0)


def ring_first(far, ring):
    axes, up, down = ring
    half = far.shape[0] // 2
    return lax.ppermute(far[:half], axes, up), lax.ppermute(far[half:], axes, down)


def ring_pair(right, left, arrived, wire):
    pack, unpack = wire
    from_up, from_down = arrived
    half = right.shape[0] // 2
    right = jnp.concatenate([pack(unpack(right[:half]) + unpack(from_up)), right[half:]], 0)
    left = jnp.concatenate([left[:half], pack(unpack(left[half:]) + unpack(from_down))], 0)
    return right, left


def ring_send(pair, ring):
    axes, up, down = ring
    return lax.ppermute(pair[0], axes, up), lax.ppermute(pair[1], axes, down)


def ring_total(own, arrived, wire):
    _, unpack = wire
    return unpack(own) + (unpack(arrived[0]) + unpack(arrived[1]))


def ring_scatter(parts, ring, wire):
    own, right, far, left = parts
    arrived = ring_send(ring_pair(right, left, ring_first(far, ring), wire), ring)
    return ring_total(own, arrived, wire)


def ring_gather(mine, ring):
    axes, up, down = ring
    half = mine.shape[0] // 2
    left = lax.ppermute(mine, axes, up)
    right = lax.ppermute(mine, axes, down)
    far_low = lax.ppermute(left[:half], axes, up)
    far_high = lax.ppermute(right[half:], axes, down)
    return [mine, right, far_low, far_high, left]


def quarters(array):
    size = array.shape[0] // SIDE
    return [array[k * size : (k + 1) * size] for k in range(SIDE)]


def join(lines):
    pieces = [piece for line in lines for piece in line]

    def kernel(*refs):
        top, k = 0, 0
        for line in lines:
            side = 0
            for piece in line:
                height, width = piece.shape
                refs[-1][top : top + height, side : side + width] = refs[k][...]
                side, k = side + width, k + 1
            top += line[0].shape[0]

    total = sum(line[0].shape[0] for line in lines)
    width = sum(piece.shape[1] for piece in lines[0])
    return pl.pallas_call(
        kernel,
        out_shape=jax.ShapeDtypeStruct((total, width), pieces[0].dtype),
        in_specs=[pl.BlockSpec(memory_space=pltpu.VMEM)] * len(pieces),
        out_specs=pl.BlockSpec(memory_space=pltpu.VMEM),
        compiler_params=pltpu.CompilerParams(vmem_limit_bytes=24 * 2**20),
    )(*pieces)


def arrange(pieces, places, which, size):
    width = pieces[0].shape[1]
    total = sum(piece.shape[0] for piece in pieces)

    def kernel(places_ref, *refs):
        out = refs[-1]
        block = 0
        for ref in refs[:-1]:
            for start in range(0, ref.shape[0], size):
                at = pl.multiple_of(places_ref[which, block] * size, size)
                out[pl.ds(at, size), :] = ref[start : start + size, :]
                block += 1

    return pl.pallas_call(
        kernel,
        out_shape=jax.ShapeDtypeStruct((total, width), pieces[0].dtype),
        in_specs=[pl.BlockSpec(memory_space=pltpu.SMEM)]
        + [pl.BlockSpec(memory_space=pltpu.VMEM)] * len(pieces),
        out_specs=pl.BlockSpec(memory_space=pltpu.VMEM),
        compiler_params=pltpu.CompilerParams(vmem_limit_bytes=24 * 2**20),
    )(places, *pieces)


def columns(array):
    size = array.shape[1] // HALVES
    return [array[:, c * size : (c + 1) * size] for c in range(HALVES)]


def after(values, done):
    return lax.optimization_barrier((values, done))[0]


def cut(left, right):
    half = left.shape[0] // 2

    def kernel(left_ref, right_ref, low_ref, high_ref):
        low_ref[...] = left_ref[:half, :]
        high_ref[...] = right_ref[half:, :]

    piece = jax.ShapeDtypeStruct((half, left.shape[1]), left.dtype)
    return pl.pallas_call(
        kernel,
        out_shape=[piece, piece],
        in_specs=[pl.BlockSpec(memory_space=pltpu.VMEM)] * 2,
        out_specs=[pl.BlockSpec(memory_space=pltpu.VMEM)] * 2,
        compiler_params=pltpu.CompilerParams(vmem_limit_bytes=24 * 2**20),
    )(left, right)


def plane_scatter(left, product, wire):
    pack, unpack = wire
    axes, up, down = PLANE_A
    blocks = quarters(left)
    far = pack(product(blocks[2]))
    half = far.shape[0] // 2
    low, high = lax.optimization_barrier((columns(far[:half]), columns(far[half:])))
    first = [(lax.ppermute(l, axes, up), lax.ppermute(h, axes, down)) for l, h in zip(low, high)]
    near = after((blocks[1], blocks[3]), low)
    right, left = [columns(pack(product(block))) for block in near]
    pairs = []
    for c in range(HALVES):
        came = first[c]
        if c:
            came = after(came, pairs[0])
        pairs.append(ring_pair(right[c], left[c], came, wire))
    second = [ring_send(pair, PLANE_A) for pair in pairs]
    own = columns(pack(product(after(blocks[0], pairs[1]))))
    sums, parts = [], None
    for c in range(HALVES):
        here = second[c]
        if parts is not None:
            here = after(here, parts)
        parts = [pack(block) for block in quarters(ring_total(own[c], here, wire))]
        _, up, down = PLANE_B
        arrived = [
            lax.ppermute(parts[k], BOTH, p) for k, p in ((2, PLANE_FAR), (1, up), (3, down))
        ]
        sums.append(unpack(parts[0]) + (unpack(arrived[0]) + (unpack(arrived[1]) + unpack(arrived[2]))))
    return sums


def plane_gather(mines, product, extra=None):
    owns, lefts, rights, halves = [], [], [], []
    axes, up, down = PLANE_A
    for mine in mines:
        far = lax.ppermute(mine, BOTH, PLANE_FAR)
        left, right = lax.ppermute(mine, BOTH, PLANE_B[1]), lax.ppermute(mine, BOTH, PLANE_B[2])
        owns.append(join([[mine], [right], [far], [left]]))
        lefts.append(lax.ppermute(owns[-1], axes, up))
        rights.append(lax.ppermute(owns[-1], axes, down))
        if extra is not None:
            lefts[-1], rights[-1], extra = lax.optimization_barrier((lefts[-1], rights[-1], extra))
        halves.append(cut(lefts[-1], rights[-1]))
    fars = [(lax.ppermute(l, axes, up), lax.ppermute(h, axes, down)) for l, h in halves]
    own = join([owns])
    product_own = product(own)
    lefts, rights = after((lefts, rights), halves[1])
    right, left = join([rights]), join([lefts])
    product_right, product_left = product(right), product(left)
    far = join(list(zip(*fars)))
    blocks = [own, right, far, left]
    return blocks, [product_own, product_right, product(far), product_left], extra


class Place:
    def __init__(self):
        row, col = lax.axis_index("row"), lax.axis_index("col")
        self.x, self.core = row // 2, row % 2
        y, z = col // 4, col % 4
        self.a = jnp.where(self.core == 0, y, z)
        self.b = jnp.where(self.core == 0, z, y)
        steps = jnp.arange(SIDE)
        halves = jnp.arange(2)

        def gather_places(core):
            step_a = (self.x + steps[:, None] - self.a + SIDE) % SIDE
            step_b = (2 * core + halves[None, :] - self.b + SIDE) % SIDE
            return (step_a * SIDE + step_b).reshape(-1)

        gather = jnp.concatenate([gather_places(self.core), gather_places(1 - self.core)])
        at_a = (self.a + steps[:, None]) % SIDE
        at_b = (self.b + steps[None, :]) % SIDE
        chip = (at_a - self.x + SIDE) % SIDE
        scatter = jnp.where(at_b // 2 == self.core, 0, 8) + chip * 2 + at_b % 2
        self.table = lax.optimization_barrier(
            jnp.stack([gather, scatter.reshape(-1)]).astype(jnp.int32)
        )


def row_gather(mine, place):
    own = ring_gather(mine, CHIPS)
    other = lax.ppermute(jnp.concatenate(own, 0), "row", SWAP)
    return arrange(own + [other], place.table, 0, mine.shape[0] // 2)


def row_scatter(pieces, place, wire):
    pack, unpack = wire
    total = sum(piece.shape[0] for piece in pieces)
    placed = arrange(pieces, place.table, 1, total // 16)
    own, other = placed[: total // 2], placed[total // 2 :]
    got = lax.ppermute(pack(other), "row", SWAP)
    own = pack(own.astype(F32) + unpack(got))
    return ring_scatter(quarters(own), CHIPS, wire)


def gelu_tanh(values):
    return jax.nn.gelu(values, approximate=True)


def rows_by(left, right):
    return jnp.dot(left, right, preferred_element_type=F32)


def against_rows(left, right):
    return lax.dot_general(left, right, (((1,), (1,)), ((), ())), preferred_element_type=F32)


def over_tokens(left, right):
    return lax.dot_general(left, right, (((0,), (0,)), ((), ())), preferred_element_type=F32)


def probabilities_difference(logits, student):
    def stats(values):
        peak = jnp.max(values, axis=1)
        return peak, jnp.sum(jnp.exp(values - peak[:, None]), axis=1)

    n = logits.shape[0]
    sent = jnp.stack([*stats(logits), *stats(student)])
    sent = jnp.broadcast_to(sent[None], (16, 4, n))
    seen = lax.all_to_all(sent, "col", 0, 0, tiled=True)

    def probability(values, peaks, sums):
        peak = jnp.max(peaks, axis=0)
        mass = jnp.sum(sums * jnp.exp(peaks - peak[None, :]), axis=0)
        return jnp.exp(values - peak[:, None]) / mass[:, None]

    return probability(logits, seen[:, 0], seen[:, 1]) - probability(student, seen[:, 2], seen[:, 3])


def local(inputs, w_up, bias_up, w_down, bias_down, student):
    place = Place()
    tokens = row_gather(inputs, place)
    preact = plane_scatter(tokens, lambda left: rows_by(left, w_up), PREACT_WIRE)
    preact = [part + bias for part, bias in zip(preact, columns(bias_up[None, :]))]
    hidden, mixed, _ = plane_gather(
        [gelu_tanh(part).astype(BF) for part in preact], lambda left: rows_by(left, w_down)
    )
    mixed_out = row_scatter(mixed, place, MIXED_WIRE)
    logits = inputs.astype(F32) + mixed_out + bias_down[None, :]
    cotangent = (D * probabilities_difference(logits, student)).astype(BF)
    slopes = row_gather(cotangent, place)
    grad_hidden = plane_scatter(slopes, lambda left: against_rows(left, w_down), GRAD_WIRE)
    grad_down = over_tokens(join([[block] for block in hidden]), slopes).astype(BF)
    grad_pre = [
        jax.vjp(gelu_tanh, part)[1](grad)[0].astype(BF) for part, grad in zip(preact, grad_hidden)
    ]
    grad_pre, back, grad_down = plane_gather(
        grad_pre, lambda left: against_rows(left, w_up).astype(BF), grad_down
    )
    grad_inputs = cotangent.astype(F32) + row_scatter(back, place, BACK_WIRE)
    grad_up = over_tokens(tokens, jnp.concatenate(grad_pre, 0)).astype(BF)
    return (grad_inputs, grad_up, grad_down)


def solution(mesh):
    return jax.shard_map(
        local,
        mesh=mesh,
        in_specs=(
            P("row", "col"),
            P("col", "row"),
            P("row"),
            P("row", "col"),
            P("col"),
            P("row", "col"),
        ),
        out_specs=(P("row", "col"), P("col", "row"), P("row", "col")),
        check_vma=False,
    )
```
